32 devices in a mesh: pix: 4 (over z), cell: 8 (over y, x, core).
Axes of the slice: x: 2, y: 2, z: 4, core: 2. Of those that a mesh axis runs over, the one named last changes fastest.
Arguments:
- influence: float32 [32768, 16384], P('pix', 'cell'), as said below
- observed: float32 [32768, 128], P(('pix', 'cell')), may hold values from -6 to 6
Outputs:
- power: float32 [16384, 128], P(('cell', 'pix'))
- residual: float32 [32768, 128], P(('pix', 'cell'))
- gradient: float32 [16384, 128], P(('cell', 'pix'))
The draws below stay inside these ranges and needn't reach their ends.
Inputs may be any that keep to these rules, and one draw needn't show every extreme that they name: A dense influence matrix with independent entries.
All inputs are finite; a program needn't handle non-finite values.
Results may differ from the reference program's by a relative error of at most 0.0003.
Values sent between devices are 32-bit elements; how exact they have to be, the bound alone decides.
No kernel may reach another device: no remote copies, remote signals or barrier semaphores. Data moves between devices by JAX's collectives and lax.ppermute only.
A program may use at most 128 MiB of HBM per device.

```python
import math
import jax
import jax.numpy as jnp
from jax import lax

M = 32768
N = 16384
F = 128
ITERS = 2


def draw_influence(key, part):
    key = jax.random.fold_in(key, 11)
    key_rows, key_cols, key_vals = jax.random.split(key, 3)
    row_trend = 3.0 ** (jnp.arange(M, dtype=jnp.float32) / M - 0.5)
    col_trend = 3.0 ** (jnp.arange(N, dtype=jnp.float32) / N - 0.5)
    row_scale = jnp.exp(jax.random.uniform(key_rows, (M, 1), jnp.float32, math.log(0.3), math.log(3.0)))
    col_scale = jnp.exp(jax.random.uniform(key_cols, (1, N), jnp.float32, math.log(0.3), math.log(3.0)))
    values = jax.random.normal(key_vals, (M, N), jnp.float32)
    return values * (row_scale * row_trend[:, None]) * (col_scale * col_trend[None, :]) / math.sqrt(N)


def level_of(key, shape, shards, smallest, high):
    def one(dim, blocks):
        draws = jax.random.uniform(jax.random.fold_in(jax.random.fold_in(key, 6), dim), (blocks,), jnp.float32, smallest / len(shards), high / len(shards))
        return jnp.repeat(jnp.exp(draws), shape[dim] // blocks).reshape((-1,) + (1,) * (len(shape) - dim - 1))

    loudness = one(*shards[0])
    for cut in shards[1:]:
        loudness = loudness * one(*cut)
    return loudness


def scatter_about(key, dims, deviation, most, pieces=(), kind=jnp.bfloat16):
    array = jax.random.normal(key, dims, jnp.float32) * deviation
    if len(pieces) > 0:
        array = level_of(key, dims, pieces, -0.22, 0.18) * array
    return jnp.clip(array, min=-most, max=most).astype(kind)


def setup_inputs(seed: int = 0) -> dict:
    key_list = jax.random.split(jax.random.key(seed), 3)
    return {
        "influence": draw_influence(jax.random.fold_in(key_list[2], 71), 0),
        "observed": scatter_about(key_list[1], (M, F), 1.0, 6.0, ((0, 32),), jnp.float32),
    }


def reference(influence, observed):
    high = lax.Precision.HIGHEST
    residual = observed
    gradient = lax.dot_general(influence, residual, (((0,), (0,)), ((), ())), precision=high, preferred_element_type=jnp.float32)
    gamma = jnp.sum(gradient * gradient, axis=0)
    direction = gradient
    power = jnp.zeros_like(gradient)
    for step in range(ITERS):
        image = jnp.dot(influence, direction, precision=high, preferred_element_type=jnp.float32)
        alpha = gamma / jnp.sum(image * image, axis=0)
        power = power + alpha * direction
        residual = residual - alpha * image
        gradient = lax.dot_general(influence, residual, (((0,), (0,)), ((), ())), precision=high, preferred_element_type=jnp.float32)
        fresh = jnp.sum(gradient * gradient, axis=0)
        direction = gradient + (fresh / gamma) * direction
        gamma = fresh
    return power, residual, gradient
```

```python
import functools

import jax
import jax.numpy as jnp
from jax import lax
from jax.experimental import pallas as pl
from jax.experimental.pallas import tpu as pltpu
from jax.sharding import PartitionSpec as P

ITERS = 2
BLOCK_ROWS = 512
VMEM_LIMIT = 50 * 2**20
f32 = jnp.float32
bf16 = jnp.bfloat16


def split(x):
    high = x.astype(bf16)
    return high, (x - high.astype(f32)).astype(bf16)


def block_rows(chunk_rows):
    return min(BLOCK_ROWS, chunk_rows)


def cost(products, rows, cols, frames):
    return pl.CostEstimate(
        flops=2 * 3 * products * rows * cols * frames,
        bytes_accessed=4 * products * rows * cols,
        transcendentals=0,
    )


def forward_kernel(parts, per_chunk, index_ref, *refs):
    x_refs, a_ref, out_ref, cat_ref, sum_ref = refs[:parts], refs[parts], refs[parts + 1], refs[parts + 2], refs[parts + 3]
    step = pl.program_id(0)
    frames = x_refs[0].shape[1]
    cells = x_refs[0].shape[0]

    @pl.when(step == 0)
    def _():
        total = jnp.zeros((1, frames), f32)
        for part in range(parts):
            x = x_refs[part][...]
            high, low = split(x)
            start = pl.multiple_of((index_ref[0] ^ part) * cells, cells)
            cat_ref[pl.ds(start, cells), :frames] = high
            cat_ref[pl.ds(start, cells), frames:] = low
            total = total + jnp.sum(x * x, axis=0, keepdims=True)
        sum_ref[...] = jnp.broadcast_to(total, sum_ref.shape)

    high, low = split(a_ref[...])
    both = jnp.dot(high, cat_ref[...], preferred_element_type=f32)
    rows = a_ref.shape[0]
    value = both[:, :frames] + both[:, frames:] + jnp.dot(low, cat_ref[:, :frames], preferred_element_type=f32)
    if per_chunk == 1:
        out_ref[0, :rows, :] = value
    else:
        start = pl.multiple_of(lax.rem(step, per_chunk) * rows, rows)
        out_ref[0, pl.ds(start, rows), :] = value
    out_ref[0, rows * per_chunk :, :] = sum_ref[...]


def forward_call(influence, x_parts, me_pix, chunks, chunk_rows):
    count = chunks.shape[0]
    cols = influence.shape[1]
    frames = x_parts[0].shape[1]
    rows = block_rows(chunk_rows)
    per_chunk = chunk_rows // rows
    index = jnp.concatenate([me_pix[None], chunks]).astype(jnp.int32)
    whole = pl.BlockSpec(memory_space=pltpu.VMEM)
    return pl.pallas_call(
        functools.partial(forward_kernel, len(x_parts), per_chunk),
        grid_spec=pltpu.PrefetchScalarGridSpec(
            num_scalar_prefetch=1,
            grid=(count * per_chunk,),
            in_specs=[whole] * len(x_parts)
            + [pl.BlockSpec((rows, cols), lambda s, ix: (ix[1 + s // per_chunk] * per_chunk + s % per_chunk, 0))],
            out_specs=pl.BlockSpec((1, chunk_rows + 8, frames), lambda s, ix: (s // per_chunk, 0, 0)),
            scratch_shapes=[pltpu.VMEM((cols, 2 * frames), bf16), pltpu.VMEM((8, frames), f32)],
        ),
        out_shape=jax.ShapeDtypeStruct((count, chunk_rows + 8, frames), f32),
        compiler_params=pltpu.CompilerParams(vmem_limit_bytes=VMEM_LIMIT),
        cost_estimate=cost(count, chunk_rows, cols, frames),
        name="forward_product",
    )(index, *x_parts, influence)


def adjoint_kernel(count, per_chunk, first, last, parts, index_ref, *refs):
    r_refs = refs[:count]
    a_ref = refs[count]
    refs = refs[count + 1 :]
    if not first:
        acc_in, sum_in = refs[0], refs[1]
        refs = refs[2:]
    if last:
        out_ref, acc, sums, cat_ref, flat = refs
    else:
        acc, sums, cat_ref = refs
    step = pl.program_id(0)
    frames = r_refs[0].shape[1]
    rows = a_ref.shape[0]

    @pl.when(step == 0)
    def _():
        total = jnp.zeros((1, frames), f32)
        for i in range(count):
            r = r_refs[i][...]
            total = total + jnp.sum(r * r, axis=0, keepdims=True)
            for k in range(per_chunk):
                high, low = split(r[k * rows : (k + 1) * rows].T)
                cat_ref[i * per_chunk + k, :frames, :] = high
                cat_ref[i * per_chunk + k, frames:, :] = low
        if first:
            sums[...] = jnp.broadcast_to(total, sums.shape)
            acc[...] = jnp.zeros_like(acc)
        else:
            sums[...] = sum_in[...] + total
            acc[...] = acc_in[...]

    high, low = split(a_ref[...])
    both = jnp.dot(cat_ref[step], high, preferred_element_type=f32)
    other = jnp.dot(cat_ref[step, :frames, :], low, preferred_element_type=f32)
    acc[...] += both[:frames] + both[frames:] + other

    if last:

        @pl.when(step == count * per_chunk - 1)
        def _():
            cells = out_ref.shape[1] - 8
            flat[...] = acc[...].T
            for part in range(parts):
                start = pl.multiple_of((index_ref[0] ^ part) * cells, cells)
                out_ref[part, :cells, :] = flat[pl.ds(start, cells), :]
                out_ref[part, cells:, :] = sums[...]


def adjoint_call(influence, r_parts, me_pix, chunks, carry, last, parts):
    count = len(r_parts)
    cols = influence.shape[1]
    chunk_rows, frames = r_parts[0].shape
    rows = block_rows(chunk_rows)
    per_chunk = chunk_rows // rows
    index = jnp.concatenate([me_pix[None], chunks]).astype(jnp.int32)
    whole = pl.BlockSpec(memory_space=pltpu.VMEM)
    cat = pltpu.VMEM((count * per_chunk, 2 * frames, rows), bf16)
    carried = (jax.ShapeDtypeStruct((frames, cols), f32), jax.ShapeDtypeStruct((8, frames), f32))
    if last:
        out_shape = jax.ShapeDtypeStruct((parts, cols // parts + 8, frames), f32)
        out_specs = whole
        scratch = [pltpu.VMEM(c.shape, f32) for c in carried] + [cat, pltpu.VMEM((cols, frames), f32)]
    else:
        out_shape = carried
        out_specs = (whole, whole)
        scratch = [cat]
    return pl.pallas_call(
        functools.partial(adjoint_kernel, count, per_chunk, carry is None, last, parts),
        grid_spec=pltpu.PrefetchScalarGridSpec(
            num_scalar_prefetch=1,
            grid=(count * per_chunk,),
            in_specs=[whole] * count
            + [pl.BlockSpec((rows, cols), lambda s, ix: (ix[1 + s // per_chunk] * per_chunk + s % per_chunk, 0))]
            + [whole] * (0 if carry is None else 2),
            out_specs=out_specs,
            scratch_shapes=scratch,
        ),
        out_shape=out_shape,
        compiler_params=pltpu.CompilerParams(vmem_limit_bytes=VMEM_LIMIT),
        cost_estimate=cost(count, chunk_rows, cols, frames),
        name="adjoint_product",
    )(index, *r_parts, influence, *(() if carry is None else carry))


def solution(mesh):
    cell_size, pix_size = mesh.shape["cell"], mesh.shape["pix"]
    bits = cell_size.bit_length() - 1
    stages = bits - 1
    group = cell_size // 2
    order = (list(range(1, bits)), list(range(bits - 1, 0, -1)))

    def offset(core, w):
        return sum(1 << order[core][j] for j in range(stages) if (w >> (stages - 1 - j)) & 1)

    offsets = [[offset(core, w) for w in range(group)] for core in range(2)]
    stage_perm = [[(i, i ^ (1 << order[i & 1][j])) for i in range(cell_size)] for j in range(stages)]
    core_perm = [(i, i ^ 1) for i in range(cell_size)]

    def body(influence, observed):
        chunk_rows = influence.shape[0] // cell_size
        me_cell, me_pix = lax.axis_index("cell"), lax.axis_index("pix")
        even = (me_cell & 1) == 0
        table = jnp.array(offsets, jnp.int32)
        own = me_cell ^ jnp.where(even, table[0], table[1])
        other = (me_cell ^ 1) ^ jnp.where(even, table[1], table[0])

        def adjoint(residual):
            mine = [residual]
            waves = []
            for j in reversed(range(stages)):
                mine = mine + [lax.ppermute(piece, "cell", stage_perm[j]) for piece in mine]
            theirs = [lax.ppermute(piece, "cell", core_perm) for piece in mine]
            cuts = [0, 1, max(1, group - 1), group]
            carry = None
            for lo, hi in zip(cuts[:-1], cuts[1:]):
                if lo == hi:
                    continue
                last = hi == group
                carry = adjoint_call(
                    influence,
                    mine[lo:hi] + theirs[lo:hi],
                    me_pix,
                    jnp.concatenate([own[lo:hi], other[lo:hi]]),
                    carry,
                    last,
                    pix_size,
                )
            total = carry[0]
            for part in range(1, pix_size):
                total = total + lax.ppermute(carry[part], "pix", [(i, i ^ part) for i in range(pix_size)])
            return total[:-8], total[-8]

        def forward(gradient):
            parts = [gradient] + [
                lax.ppermute(gradient, "pix", [(i, i ^ part) for i in range(pix_size)]) for part in range(1, pix_size)
            ]
            call = functools.partial(forward_call, influence, parts, me_pix)
            sent = lax.ppermute(call(other, chunk_rows), "cell", core_perm)
            half = group // 2
            away, home = call(own[half:], chunk_rows), call(own[:half], chunk_rows)
            away, home = away + sent[half:], home + sent[:half]
            for j in range(stages):
                home = home + lax.ppermute(away, "cell", stage_perm[j])
                half = home.shape[0] // 2
                away, home = home[half:], home[: max(half, 1)]
            return home[0, :-8], home[0, -8]

        gradient, _ = adjoint(observed)
        image, gamma = forward(gradient)
        direction = gradient
        residual = observed
        power = jnp.zeros_like(gradient)
        for step in range(ITERS):
            back, squares = adjoint(image)
            alpha = gamma / squares
            power = power + alpha * direction
            residual = residual - alpha * image
            gradient = gradient - alpha * back
            if step + 1 < ITERS:
                fresh_image, fresh = forward(gradient)
                beta = fresh / gamma
                image = fresh_image + beta * image
                direction = gradient + beta * direction
                gamma = fresh
        return (power, residual, gradient)

    in_specs = (P("pix", "cell"), P(("pix", "cell"), None))
    out_specs = (P(("cell", "pix"), None), P(("pix", "cell"), None), P(("cell", "pix"), None))
    return jax.shard_map(body, mesh=mesh, in_specs=in_specs, out_specs=out_specs, check_vma=False)
```

```python
import functools

import jax
import jax.numpy as jnp
from jax import lax
from jax.experimental import pallas as pl
from jax.experimental.pallas import tpu as pltpu
from jax.sharding import PartitionSpec as P

ITERS = 2
BLOCK_ROWS = 512
FIRST_LIMIT = 18 * 2**20
LATER_LIMIT = 8 * 2**20
f32 = jnp.float32
bf16 = jnp.bfloat16
f8 = jnp.float8_e4m3fn
RANGE = 224.0 * 256.0
VMEM = pl.BlockSpec(memory_space=pltpu.VMEM)
SMEM = pl.BlockSpec(memory_space=pltpu.SMEM)


def resident(x):
    return pltpu.with_memory_space_constraint(x, pltpu.VMEM)


def split(x):
    high = x.astype(bf16)
    return high, (x - high.astype(f32)).astype(bf16)


def squares(x):
    return jnp.sum(x * x, axis=0, keepdims=True)


def cost(rows, cols, frames, width):
    return pl.CostEstimate(flops=2 * 3 * rows * cols * frames, bytes_accessed=width * rows * cols, transcendentals=0)


def emit_parts(pix, acc, sums, flat_ref, out_ref):
    parts = out_ref.shape[0]
    cells = out_ref.shape[1] - 8
    flat_ref[...] = acc.T
    for part in range(parts):
        start = pl.multiple_of(((pix & (parts - 1)) ^ part) * cells, cells)
        out_ref[part, :cells, :] = flat_ref[pl.ds(start, cells), :]
        out_ref[part, cells:, :] = sums


def first_kernel(count, per_chunk, first, last, index_ref, *refs):
    r_refs, refs = refs[:count], refs[count:]
    near_ref, far_ref, refs = refs[0], refs[1], refs[2:]
    if not first:
        (near_in, far_in, sum_in), refs = refs[:3], refs[3:]
    high_refs, low_refs, scale_ref, refs = refs[:2], refs[2:4], refs[4], refs[5:]
    if last:
        near_out, far_out, near, far, sums, cat_ref, flat_ref = refs
    else:
        near, far, sums, cat_ref = refs
    step = pl.program_id(0)
    frames = r_refs[0].shape[1]
    rows, half = near_ref.shape

    @pl.when(step == 0)
    def _():
        total = jnp.zeros((1, frames), f32)
        for i in range(count):
            r = r_refs[i][...]
            total = total + squares(r)
            for k in range(per_chunk):
                high, low = split(r[k * rows : (k + 1) * rows].T)
                cat_ref[i * per_chunk + k, :frames, :] = high
                cat_ref[i * per_chunk + k, frames:, :] = low
        if first:
            sums[...] = jnp.broadcast_to(total, sums.shape)
            near[...] = jnp.zeros_like(near)
            far[...] = jnp.zeros_like(far)
        else:
            sums[...] = sum_in[...] + total
            near[...] = near_in[...]
            far[...] = far_in[...]

    here = pl.ds(pl.multiple_of(step * rows, rows), rows)
    for k, (ref, acc) in enumerate(((near_ref, near), (far_ref, far))):
        value = ref[...]
        high = value.astype(bf16)
        low = value - high.astype(f32)
        largest = jnp.maximum(jnp.max(jnp.max(jnp.abs(high), axis=0, keepdims=True).astype(f32)), 1e-30)
        high_refs[k][here, :] = high
        low_refs[k][...] = (low * (RANGE / largest)).astype(f8)
        scale_ref[step, k] = largest * (1.0 / RANGE)
        both = jnp.dot(cat_ref[step], high, preferred_element_type=f32)
        other = jnp.dot(cat_ref[step, :frames, :], low.astype(bf16), preferred_element_type=f32)
        acc[...] += both[:frames] + both[frames:] + other

    if last:

        @pl.when(step == count * per_chunk - 1)
        def _():
            emit_parts(index_ref[0], near[...], sums[...], flat_ref, near_out)
            emit_parts(index_ref[0], far[...], sums[...], flat_ref, far_out)


def blocks(rows, half, per_chunk, base):
    def block(far):
        def where(s, ix):
            return (ix[2 + base + s // per_chunk] * per_chunk + s % per_chunk, ix[1] ^ far)

        return pl.BlockSpec((rows, half), where)

    return [block(0), block(1)]


def first_call(influence, r_parts, index, base, carry, last, parts):
    count = len(r_parts)
    cols = influence.shape[1]
    half = cols // 2
    chunk_rows, frames = r_parts[0].shape
    rows = min(BLOCK_ROWS, chunk_rows)
    per_chunk = chunk_rows // rows
    accs = [((frames, half), f32)] * 2 + [((8, frames), f32)]
    cat = pltpu.VMEM((count * per_chunk, 2 * frames, rows), bf16)
    out_shape = [
        *[pltpu.VMEM((count * chunk_rows, half), bf16)] * 2,
        *[pltpu.HBM((count * chunk_rows, half), f8)] * 2,
        jax.ShapeDtypeStruct((count * per_chunk, 2), f32),
    ]
    if last:
        out_shape += [jax.ShapeDtypeStruct((parts // 2, half // (parts // 2) + 8, frames), f32)] * 2
        scratch = [pltpu.VMEM(*a) for a in accs] + [cat, pltpu.VMEM((half, frames), f32)]
    else:
        out_shape += [jax.ShapeDtypeStruct(*a) for a in accs]
        scratch = [cat]
    high_near, high_far, low_near, low_far, scale, *rest = pl.pallas_call(
        functools.partial(first_kernel, count, per_chunk, carry is None, last),
        grid_spec=pltpu.PrefetchScalarGridSpec(
            num_scalar_prefetch=1,
            grid=(count * per_chunk,),
            in_specs=[VMEM] * count + blocks(rows, half, per_chunk, base) + [VMEM] * (0 if carry is None else 3),
            out_specs=[VMEM] * 2 + [pl.BlockSpec((rows, half), lambda s, ix: (s, 0))] * 2 + [SMEM] + [VMEM] * (len(out_shape) - 5),
            scratch_shapes=scratch,
        ),
        out_shape=out_shape,
        compiler_params=pltpu.CompilerParams(vmem_limit_bytes=FIRST_LIMIT),
        cost_estimate=cost(count * chunk_rows, cols, frames, 4),
        name="first_adjoint",
    )(index, *r_parts, influence, influence, *(() if carry is None else carry))
    return (high_near, high_far), (low_near, low_far, scale), rest


def adjoint_kernel(count, sides, last, index_ref, *refs):
    halves = len(sides)
    r_refs, refs = refs[:count], refs[count:]
    high_refs, low_refs, scale_ref, refs = refs[:halves], refs[halves : 2 * halves], refs[2 * halves], refs[2 * halves + 1 :]
    accs_in, sum_in, refs = refs[:halves], refs[halves], refs[halves + 1 :]
    if last:
        outs, refs = refs[:1], refs[1:]
    else:
        outs, sum_out, refs = refs[:halves], refs[halves], refs[halves + 1 :]
    cat_ref, scaled_ref = refs[:2]
    chunk_rows, frames = r_refs[0].shape
    rows = cat_ref.shape[1] // scale_ref.shape[0]
    total = sum_in[...]
    for i in range(count):
        r = r_refs[i][...]
        total = total + squares(r)
        turned = r.T
        high, low = split(turned)
        here = slice(i * chunk_rows, (i + 1) * chunk_rows)
        cat_ref[:frames, here] = high
        cat_ref[frames:, here] = low
        for b in range(chunk_rows // rows):
            at = i * chunk_rows + b * rows
            for k in range(halves):
                scale = scale_ref[at // rows, sides[k]]
                scaled_ref[k, :, at : at + rows] = (turned[:, b * rows : (b + 1) * rows] * scale).astype(bf16)
    for k in range(halves):
        both = jnp.dot(cat_ref[...], high_refs[k][...], preferred_element_type=f32)
        acc = accs_in[k][...] + both[:frames] + both[frames:]
        acc = acc + jnp.dot(scaled_ref[k], low_refs[k][...].astype(bf16), preferred_element_type=f32)
        if last:
            emit_parts(index_ref[0], acc, total, refs[2], outs[0])
        else:
            outs[k][...] = acc
    if not last:
        sum_out[...] = total


def adjoint_call(high, low, r_parts, index, carry, sides, last, parts):
    count = len(r_parts)
    rows = high[0].shape[0]
    halves = len(sides)
    half = carry[0].shape[1]
    frames = r_parts[0].shape[1]
    scratch = [
        pltpu.VMEM((2 * frames, rows), bf16),
        pltpu.VMEM((halves, frames, rows), bf16),
    ]
    if last:
        out_shape = jax.ShapeDtypeStruct((parts // 2, half // (parts // 2) + 8, frames), f32)
        out_specs = VMEM
        scratch.append(pltpu.VMEM((half, frames), f32))
    else:
        out_shape = [jax.ShapeDtypeStruct(c.shape, f32) for c in carry]
        out_specs = [VMEM] * (halves + 1)
    return pl.pallas_call(
        functools.partial(adjoint_kernel, count, sides, last),
        in_specs=[SMEM] + [VMEM] * (count + 2 * halves) + [SMEM] + [VMEM] * (halves + 1),
        out_specs=out_specs,
        out_shape=out_shape,
        scratch_shapes=scratch,
        compiler_params=pltpu.CompilerParams(vmem_limit_bytes=LATER_LIMIT),
        cost_estimate=cost(rows, halves * half, frames, 2),
        name="adjoint_product",
    )(
        index,
        *r_parts,
        *[resident(high[k]) for k in sides],
        *[resident(low[k]) for k in sides],
        low[2],
        *carry,
    )


def forward_kernel(parts, arrays, places, side, chunk_rows, near, index_ref, *refs):
    x_refs, refs = refs[:parts], refs[parts:]
    highs, lows, scales, refs = refs[:arrays], refs[arrays : 2 * arrays], refs[2 * arrays : 3 * arrays], refs[3 * arrays :]
    count = len(places)
    if not near:
        added, sum_in, refs = refs[:count], refs[count], refs[count + 1 :]
    outs, refs = refs[:count], refs[count:]
    if near:
        sum_out, refs = refs[0], refs[1:]
    (cat_ref,) = refs
    cells, frames = x_refs[0].shape
    total = jnp.zeros((1, frames), f32)
    for part in range(parts):
        x = x_refs[part][...]
        high, low = split(x)
        start = pl.multiple_of(((index_ref[0] & (parts - 1)) ^ part) * cells, cells)
        cat_ref[pl.ds(start, cells), :frames] = high
        cat_ref[pl.ds(start, cells), frames:] = low
        total = total + squares(x)
    if near:
        sum_out[...] = jnp.broadcast_to(total, sum_out.shape)
    for i, (which, row) in enumerate(places):
        both = jnp.dot(highs[which][row : row + chunk_rows, :], cat_ref[...], preferred_element_type=f32)
        value = both[:, :frames] + both[:, frames:]
        other = jnp.dot(lows[which][row : row + chunk_rows, :].astype(bf16), cat_ref[:, :frames], preferred_element_type=f32)
        rows = highs[which].shape[0] // scales[which].shape[0]
        for start in range(0, chunk_rows, rows):
            at = slice(start, start + rows)
            whole = value[at] + other[at] * scales[which][(row + start) // rows, side]
            outs[i][at, :] = whole if near else whole + added[i][at, :]
        if not near:
            outs[i][chunk_rows:, :] = sum_in[...] + total


def forward_call(highs, lows, x_parts, index, places, chunk_rows, side, added):
    count = len(places)
    used = sorted({g for g, _ in places})
    slots = [(used.index(g), row) for g, row in places]
    cells, frames = x_parts[0].shape
    half = cells * len(x_parts)
    near = added is None
    extra = [] if near else [*added[0], added[1]]
    rows = chunk_rows if near else chunk_rows + 8
    out_shape = [jax.ShapeDtypeStruct((rows, frames), f32)] * count
    if near:
        out_shape.append(jax.ShapeDtypeStruct((8, frames), f32))
    return pl.pallas_call(
        functools.partial(forward_kernel, len(x_parts), len(used), slots, side, chunk_rows, near),
        in_specs=[SMEM]
        + [VMEM] * (len(x_parts) + len(used))
        + [VMEM] * len(used)
        + [SMEM] * len(used)
        + [VMEM] * len(extra),
        out_specs=[VMEM] * len(out_shape),
        out_shape=out_shape,
        scratch_shapes=[
            pltpu.VMEM((half, 2 * frames), bf16),
        ],
        compiler_params=pltpu.CompilerParams(vmem_limit_bytes=LATER_LIMIT),
        cost_estimate=cost(count * chunk_rows, half, frames, 2),
        name="forward_product",
    )(
        index,
        *x_parts,
        *[resident(highs[g][side]) for g in used],
        *[resident(lows[g][side]) for g in used],
        *[lows[g][2] for g in used],
        *extra,
    )


def solution(mesh):
    cell_size, pix_size = mesh.shape["cell"], mesh.shape["pix"]
    bits = cell_size.bit_length() - 1
    stages = bits - 1
    group = cell_size // 2
    order = (list(range(1, bits)), list(range(bits - 1, 0, -1)))

    def offset(core, w):
        return sum(1 << order[core][j] for j in range(stages) if (w >> (stages - 1 - j)) & 1)

    stage_perm = [[(i, i ^ (1 << order[i & 1][j])) for i in range(cell_size)] for j in range(stages)]
    core_perm = [(i, i ^ 1) for i in range(cell_size)]
    pix_perm = [[(i, i ^ part) for i in range(pix_size)] for part in range(pix_size)]
    middle = range(1, group - 1)
    groups = [[(0, 0), (1, 0)], [(0, w) for w in middle], [(1, w) for w in middle], [(0, group - 1), (1, group - 1)]]

    starts = [sum(map(len, groups[:g])) for g in range(len(groups))]
    uses = [[offset(core ^ c, w) ^ c for members in groups for c, w in members] for core in range(2)]

    def body(influence, observed):
        chunk_rows = influence.shape[0] // cell_size
        me_cell, me_pix = lax.axis_index("cell"), lax.axis_index("pix")
        order_of_use = jnp.where((me_cell & 1) == 0, jnp.array(uses[0], jnp.int32), jnp.array(uses[1], jnp.int32))
        index = jnp.concatenate([jnp.stack([me_pix, me_pix // (pix_size // 2)]), me_cell ^ order_of_use])
        place = {c: (g, i * chunk_rows) for g, members in enumerate(groups) for i, c in enumerate(members)}
        highs, lows = [], []

        def stage(piece, j):
            return lax.ppermute(piece, "cell", stage_perm[j])

        def flip(piece):
            return lax.ppermute(piece, "cell", core_perm)

        def between(piece, part):
            return lax.ppermute(piece, "pix", pix_perm[part])

        def adjoint(residual):
            half = influence.shape[1] // 2
            first = not highs
            carry = None if first else [
                jnp.zeros((residual.shape[1], half), f32),
                jnp.zeros((residual.shape[1], half), f32),
                jnp.zeros((8, residual.shape[1]), f32),
            ]

            def multiply(g, pieces, carry):
                if first:
                    high, low, carry = first_call(
                        influence, pieces, index, starts[g], carry, g == len(groups) - 1, pix_size
                    )
                    highs.append(high)
                    lows.append(low)
                    return carry
                if g < len(groups) - 1:
                    return adjoint_call(highs[g], lows[g], pieces, index, carry, (0, 1), False, pix_size)
                far = adjoint_call(highs[g], lows[g], pieces, index, carry[1:], (1,), True, pix_size)
                near = adjoint_call(highs[g], lows[g], pieces, index, [carry[0], carry[2]], (0,), True, pix_size)
                return near, far

            mine = [residual]
            for j in reversed(range(1, stages)):
                mine = mine + [stage(piece, j) for piece in mine]
            crossed = stage(residual, 0)
            carry = multiply(0, [residual, flip(residual)], carry)
            rest, crossed, carry = lax.optimization_barrier((mine[1:], crossed, carry))
            mine = [residual, *rest, crossed, *[stage(piece, 0) for piece in rest]]
            theirs = [None] + [flip(piece) for piece in mine[1 : group - 1]]
            carry = multiply(1, [mine[w] for w in middle], carry)
            last, carry = lax.optimization_barrier((mine[group - 1], carry))
            carry = multiply(2, [theirs[w] for w in middle], carry)
            near, far = multiply(3, [last, flip(last)], carry)
            total = near[0]
            for part in [*range(1, pix_size // 2), *range(pix_size // 2, pix_size)]:
                piece = near[part] if part < pix_size // 2 else far[part - pix_size // 2]
                total = total + between(piece, part)
            return total[:-8], total[-8]

        def forward(gradient):
            parts = [gradient] + [between(gradient, part) for part in range(1, pix_size)]
            near, far = parts[: pix_size // 2], parts[pix_size // 2 :]
            theirs = [place[1, w] for w in range(group)]
            mine = [place[0, w] for w in range(group)]
            *their_near, sums = forward_call(highs, lows, near, index, theirs, chunk_rows, 0, None)
            *mine_near, _ = forward_call(highs, lows, near, index, mine, chunk_rows, 0, None)
            half = group // 2
            far, their_near, mine_near = lax.optimization_barrier((far, their_near, mine_near))

            def finish(places, added):
                return forward_call(highs, lows, far, index, places, chunk_rows, 1, (added, sums))

            sent = flip(jnp.stack(finish(theirs, their_near)))
            away = finish(mine[half:], mine_near[half:])
            home = finish(mine[:half], mine_near[:half])
            held = [piece + sent[w] for w, piece in enumerate([*home, *away])]
            for j in range(stages):
                half = len(held) // 2
                for w in reversed(range(half)):
                    held[w] = held[w] + stage(held[w + half], j)
                held = held[:half]
            return held[0][:-8], held[0][-8]

        gradient, _ = adjoint(observed)
        image, gamma = forward(gradient)
        direction = gradient
        residual = observed
        power = jnp.zeros_like(gradient)
        for step in range(ITERS):
            back, image_squares = adjoint(image)
            alpha = gamma / image_squares
            power = power + alpha * direction
            residual = residual - alpha * image
            gradient = gradient - alpha * back
            if step + 1 < ITERS:
                fresh_image, fresh = forward(gradient)
                beta = fresh / gamma
                image = fresh_image + beta * image
                direction = gradient + beta * direction
                gamma = fresh
        return (power, residual, gradient)

    in_specs = (P("pix", "cell"), P(("pix", "cell"), None))
    out_specs = (P(("cell", "pix"), None), P(("pix", "cell"), None), P(("cell", "pix"), None))
    return jax.shard_map(body, mesh=mesh, in_specs=in_specs, out_specs=out_specs, check_vma=False)
```

```python
import functools

import jax
import jax.numpy as jnp
from jax import lax
from jax.experimental import pallas as pl
from jax.experimental.pallas import tpu as pltpu
from jax.sharding import PartitionSpec as P

ITERS = 2
BLOCK_ROWS = 512
FIRST_LIMIT = 18 * 2**20
LATER_LIMIT = 8 * 2**20
f32 = jnp.float32
bf16 = jnp.bfloat16
f8 = jnp.float8_e4m3fn
RANGE = 224.0 * 256.0
VMEM = pl.BlockSpec(memory_space=pltpu.VMEM)
SMEM = pl.BlockSpec(memory_space=pltpu.SMEM)


def resident(x):
    return pltpu.with_memory_space_constraint(x, pltpu.VMEM)


def split(x):
    high = x.astype(bf16)
    return high, (x - high.astype(f32)).astype(bf16)


def squares(x):
    return jnp.sum(x * x, axis=0, keepdims=True)


def cost(rows, cols, frames, width):
    return pl.CostEstimate(flops=2 * 3 * rows * cols * frames, bytes_accessed=width * rows * cols, transcendentals=0)


def emit_parts(pix, acc, sums, flat_ref, out_ref):
    parts = out_ref.shape[0]
    cells = out_ref.shape[1] - 8
    flat_ref[...] = acc.T
    for part in range(parts):
        start = pl.multiple_of(((pix & (parts - 1)) ^ part) * cells, cells)
        out_ref[part, :cells, :] = flat_ref[pl.ds(start, cells), :]
        out_ref[part, cells:, :] = sums


def first_kernel(count, per_chunk, first, last, index_ref, *refs):
    r_refs, refs = refs[:count], refs[count:]
    near_ref, far_ref, refs = refs[0], refs[1], refs[2:]
    if not first:
        (near_in, far_in, sum_in), refs = refs[:3], refs[3:]
    high_refs, low_refs, scale_ref, refs = refs[:2], refs[2:4], refs[4], refs[5:]
    if last:
        near_out, far_out, near, far, sums, cat_ref, flat_ref = refs
    else:
        near, far, sums, cat_ref = refs
    step = pl.program_id(0)
    frames = r_refs[0].shape[1]
    rows, half = near_ref.shape

    @pl.when(step == 0)
    def _():
        total = jnp.zeros((1, frames), f32)
        for i in range(count):
            r = r_refs[i][...]
            total = total + squares(r)
            for k in range(per_chunk):
                high, low = split(r[k * rows : (k + 1) * rows].T)
                cat_ref[i * per_chunk + k, :frames, :] = high
                cat_ref[i * per_chunk + k, frames:, :] = low
        if first:
            sums[...] = jnp.broadcast_to(total, sums.shape)
            near[...] = jnp.zeros_like(near)
            far[...] = jnp.zeros_like(far)
        else:
            sums[...] = sum_in[...] + total
            near[...] = near_in[...]
            far[...] = far_in[...]

    here = pl.ds(pl.multiple_of(step * rows, rows), rows)
    for k, (ref, acc) in enumerate(((near_ref, near), (far_ref, far))):
        value = ref[...]
        high = value.astype(bf16)
        low = value - high.astype(f32)
        largest = jnp.maximum(jnp.max(jnp.max(jnp.abs(high), axis=0, keepdims=True).astype(f32)), 1e-30)
        high_refs[k][here, :] = high
        low_refs[k][...] = (low * (RANGE / largest)).astype(f8)
        scale_ref[step, k] = largest * (1.0 / RANGE)
        both = jnp.dot(cat_ref[step], high, preferred_element_type=f32)
        other = jnp.dot(cat_ref[step, :frames, :], low.astype(bf16), preferred_element_type=f32)
        acc[...] += both[:frames] + both[frames:] + other

    if last:

        @pl.when(step == count * per_chunk - 1)
        def _():
            emit_parts(index_ref[0], near[...], sums[...], flat_ref, near_out)
            emit_parts(index_ref[0], far[...], sums[...], flat_ref, far_out)


def blocks(rows, half, per_chunk, base):
    def block(far):
        def where(s, ix):
            return (ix[2 + base + s // per_chunk] * per_chunk + s % per_chunk, ix[1] ^ far)

        return pl.BlockSpec((rows, half), where)

    return [block(0), block(1)]


def first_call(influence, r_parts, index, base, carry, last, parts):
    count = len(r_parts)
    cols = influence.shape[1]
    half = cols // 2
    chunk_rows, frames = r_parts[0].shape
    rows = min(BLOCK_ROWS, chunk_rows)
    per_chunk = chunk_rows // rows
    accs = [((frames, half), f32)] * 2 + [((8, frames), f32)]
    cat = pltpu.VMEM((count * per_chunk, 2 * frames, rows), bf16)
    out_shape = [
        *[pltpu.VMEM((count * chunk_rows, half), bf16)] * 2,
        *[pltpu.HBM((count * chunk_rows, half), f8)] * 2,
        jax.ShapeDtypeStruct((count * per_chunk, 2), f32),
    ]
    if last:
        out_shape += [jax.ShapeDtypeStruct((parts // 2, half // (parts // 2) + 8, frames), f32)] * 2
        scratch = [pltpu.VMEM(*a) for a in accs] + [cat, pltpu.VMEM((half, frames), f32)]
    else:
        out_shape += [jax.ShapeDtypeStruct(*a) for a in accs]
        scratch = [cat]
    high_near, high_far, low_near, low_far, scale, *rest = pl.pallas_call(
        functools.partial(first_kernel, count, per_chunk, carry is None, last),
        grid_spec=pltpu.PrefetchScalarGridSpec(
            num_scalar_prefetch=1,
            grid=(count * per_chunk,),
            in_specs=[VMEM] * count + blocks(rows, half, per_chunk, base) + [VMEM] * (0 if carry is None else 3),
            out_specs=[VMEM] * 2 + [pl.BlockSpec((rows, half), lambda s, ix: (s, 0))] * 2 + [SMEM] + [VMEM] * (len(out_shape) - 5),
            scratch_shapes=scratch,
        ),
        out_shape=out_shape,
        compiler_params=pltpu.CompilerParams(vmem_limit_bytes=FIRST_LIMIT),
        cost_estimate=cost(count * chunk_rows, cols, frames, 4),
        name="first_adjoint",
    )(index, *r_parts, influence, influence, *(() if carry is None else carry))
    return (high_near, high_far), (low_near, low_far, scale), rest


def adjoint_kernel(count, sides, last, index_ref, *refs):
    halves = len(sides)
    r_refs, refs = refs[:count], refs[count:]
    high_refs, low_refs, scale_ref, refs = refs[:halves], refs[halves : 2 * halves], refs[2 * halves], refs[2 * halves + 1 :]
    accs_in, sum_in, refs = refs[:halves], refs[halves], refs[halves + 1 :]
    if last:
        outs, refs = refs[:1], refs[1:]
    else:
        outs, sum_out, refs = refs[:halves], refs[halves], refs[halves + 1 :]
    cat_ref, scaled_ref = refs[:2]
    chunk_rows, frames = r_refs[0].shape
    rows = cat_ref.shape[1] // scale_ref.shape[0]
    total = sum_in[...]
    for i in range(count):
        r = r_refs[i][...]
        total = total + squares(r)
        turned = r.T
        high, low = split(turned)
        here = slice(i * chunk_rows, (i + 1) * chunk_rows)
        cat_ref[:frames, here] = high
        cat_ref[frames:, here] = low
        for b in range(chunk_rows // rows):
            at = i * chunk_rows + b * rows
            for k in range(halves):
                scale = scale_ref[at // rows, sides[k]]
                scaled_ref[k, :, at : at + rows] = (turned[:, b * rows : (b + 1) * rows] * scale).astype(bf16)
    for k in range(halves):
        both = jnp.dot(cat_ref[...], high_refs[k][...], preferred_element_type=f32)
        acc = accs_in[k][...] + both[:frames] + both[frames:]
        acc = acc + jnp.dot(scaled_ref[k], low_refs[k][...].astype(bf16), preferred_element_type=f32)
        if last:
            emit_parts(index_ref[0], acc, total, refs[2], outs[0])
        else:
            outs[k][...] = acc
    if not last:
        sum_out[...] = total


def adjoint_call(high, low, r_parts, index, carry, sides, last, parts):
    count = len(r_parts)
    rows = high[0].shape[0]
    halves = len(sides)
    half = carry[0].shape[1]
    frames = r_parts[0].shape[1]
    scratch = [
        pltpu.VMEM((2 * frames, rows), bf16),
        pltpu.VMEM((halves, frames, rows), bf16),
    ]
    if last:
        out_shape = jax.ShapeDtypeStruct((parts // 2, half // (parts // 2) + 8, frames), f32)
        out_specs = VMEM
        scratch.append(pltpu.VMEM((half, frames), f32))
    else:
        out_shape = [jax.ShapeDtypeStruct(c.shape, f32) for c in carry]
        out_specs = [VMEM] * (halves + 1)
    return pl.pallas_call(
        functools.partial(adjoint_kernel, count, sides, last),
        in_specs=[SMEM] + [VMEM] * (count + 2 * halves) + [SMEM] + [VMEM] * (halves + 1),
        out_specs=out_specs,
        out_shape=out_shape,
        scratch_shapes=scratch,
        compiler_params=pltpu.CompilerParams(vmem_limit_bytes=LATER_LIMIT),
        cost_estimate=cost(rows, halves * half, frames, 2),
        name="adjoint_product",
    )(
        index,
        *r_parts,
        *[resident(high[k]) for k in sides],
        *[resident(low[k]) for k in sides],
        low[2],
        *carry,
    )


def forward_kernel(parts, arrays, places, side, chunk_rows, near, index_ref, *refs):
    x_refs, refs = refs[:parts], refs[parts:]
    highs, lows, scales, refs = refs[:arrays], refs[arrays : 2 * arrays], refs[2 * arrays : 3 * arrays], refs[3 * arrays :]
    count = len(places)
    if not near:
        added, sum_in, refs = refs[:count], refs[count], refs[count + 1 :]
    if near:
        outs, sum_out, refs = refs[:count], refs[count], refs[count + 1 :]
    else:
        outs, refs = [refs[0].at[i] for i in range(count)], refs[1:]
    (cat_ref,) = refs
    cells, frames = x_refs[0].shape
    total = jnp.zeros((1, frames), f32)
    for part in range(parts):
        x = x_refs[part][...]
        high, low = split(x)
        start = pl.multiple_of(((index_ref[0] & (parts - 1)) ^ part) * cells, cells)
        cat_ref[pl.ds(start, cells), :frames] = high
        cat_ref[pl.ds(start, cells), frames:] = low
        total = total + squares(x)
    if near:
        sum_out[...] = jnp.broadcast_to(total, sum_out.shape)
    for i, (which, row) in enumerate(places):
        both = jnp.dot(highs[which][row : row + chunk_rows, :], cat_ref[...], preferred_element_type=f32)
        value = both[:, :frames] + both[:, frames:]
        other = jnp.dot(lows[which][row : row + chunk_rows, :].astype(bf16), cat_ref[:, :frames], preferred_element_type=f32)
        rows = highs[which].shape[0] // scales[which].shape[0]
        for start in range(0, chunk_rows, rows):
            at = slice(start, start + rows)
            whole = value[at] + other[at] * scales[which][(row + start) // rows, side]
            outs[i][at, :] = whole if near else whole + added[i][at, :]
        if not near:
            outs[i][chunk_rows:, :] = sum_in[...] + total


def forward_call(highs, lows, x_parts, index, places, chunk_rows, side, added):
    count = len(places)
    used = sorted({g for g, _ in places})
    slots = [(used.index(g), row) for g, row in places]
    cells, frames = x_parts[0].shape
    half = cells * len(x_parts)
    near = added is None
    extra = [] if near else [*added[0], added[1]]
    rows = chunk_rows if near else chunk_rows + 8
    if near:
        out_shape = [jax.ShapeDtypeStruct((rows, frames), f32)] * count + [jax.ShapeDtypeStruct((8, frames), f32)]
    else:
        out_shape = [jax.ShapeDtypeStruct((count, rows, frames), f32)]
    result = pl.pallas_call(
        functools.partial(forward_kernel, len(x_parts), len(used), slots, side, chunk_rows, near),
        in_specs=[SMEM]
        + [VMEM] * (len(x_parts) + len(used))
        + [VMEM] * len(used)
        + [SMEM] * len(used)
        + [VMEM] * len(extra),
        out_specs=[VMEM] * len(out_shape),
        out_shape=out_shape,
        scratch_shapes=[
            pltpu.VMEM((half, 2 * frames), bf16),
        ],
        compiler_params=pltpu.CompilerParams(vmem_limit_bytes=LATER_LIMIT),
        cost_estimate=cost(count * chunk_rows, half, frames, 2),
        name="forward_product",
    )(
        index,
        *x_parts,
        *[resident(highs[g][side]) for g in used],
        *[resident(lows[g][side]) for g in used],
        *[lows[g][2] for g in used],
        *extra,
    )
    return result if near else result[0]


def solution(mesh):
    cell_size, pix_size = mesh.shape["cell"], mesh.shape["pix"]
    bits = cell_size.bit_length() - 1
    stages = bits - 1
    group = cell_size // 2
    order = (list(range(1, bits)), list(range(bits - 1, 0, -1)))

    def offset(core, w):
        return sum(1 << order[core][j] for j in range(stages) if (w >> (stages - 1 - j)) & 1)

    stage_perm = [[(i, i ^ (1 << order[i & 1][j])) for i in range(cell_size)] for j in range(stages)]
    core_perm = [(i, i ^ 1) for i in range(cell_size)]
    pix_bits = pix_size.bit_length() - 1
    pix_perm = [[(i, i ^ (1 << b)) for i in range(pix_size)] for b in range(pix_bits)]
    middle = range(1, group - 1)
    groups = [[(0, 0), (1, 0)], [(0, w) for w in middle], [(1, w) for w in middle], [(0, group - 1), (1, group - 1)]]

    starts = [sum(map(len, groups[:g])) for g in range(len(groups))]
    uses = [[offset(core ^ c, w) ^ c for members in groups for c, w in members] for core in range(2)]

    def body(influence, observed):
        chunk_rows = influence.shape[0] // cell_size
        me_cell, me_pix = lax.axis_index("cell"), lax.axis_index("pix")
        order_of_use = jnp.where((me_cell & 1) == 0, jnp.array(uses[0], jnp.int32), jnp.array(uses[1], jnp.int32))
        index = jnp.concatenate([jnp.stack([me_pix, me_pix // (pix_size // 2)]), me_cell ^ order_of_use])
        place = {c: (g, i * chunk_rows) for g, members in enumerate(groups) for i, c in enumerate(members)}
        highs, lows = [], []

        def stage(piece, j):
            return lax.ppermute(piece, "cell", stage_perm[j])

        def flip(piece):
            return lax.ppermute(piece, "cell", core_perm)

        def between(piece, b):
            return lax.ppermute(piece, "pix", pix_perm[b])

        def adjoint(residual):
            half = influence.shape[1] // 2
            first = not highs
            carry = None if first else [
                jnp.zeros((residual.shape[1], half), f32),
                jnp.zeros((residual.shape[1], half), f32),
                jnp.zeros((8, residual.shape[1]), f32),
            ]

            def multiply(g, pieces, carry):
                if first:
                    high, low, carry = first_call(
                        influence, pieces, index, starts[g], carry, g == len(groups) - 1, pix_size
                    )
                    highs.append(high)
                    lows.append(low)
                    return carry
                if g < len(groups) - 1:
                    return adjoint_call(highs[g], lows[g], pieces, index, carry, (0, 1), False, pix_size)
                far = adjoint_call(highs[g], lows[g], pieces, index, carry[1:], (1,), True, pix_size)
                near = adjoint_call(highs[g], lows[g], pieces, index, [carry[0], carry[2]], (0,), True, pix_size)
                return near, far

            mine = [residual]
            for j in reversed(range(1, stages)):
                mine = mine + [stage(piece, j) for piece in mine]
            early = stage(residual, 0) if first else None
            carry = multiply(0, [residual, flip(residual)], carry)
            late, carry = lax.optimization_barrier((residual, carry))
            crossed = early if first else stage(late, 0)
            rest, carry = lax.optimization_barrier((mine[1:], carry))
            mine = [residual, *rest, crossed, *[stage(piece, 0) for piece in rest]]
            theirs = [None] + [flip(piece) for piece in mine[1 : group - 1]]
            carry = multiply(1, [mine[w] for w in middle], carry)
            last, carry = lax.optimization_barrier((mine[group - 1], carry))
            carry = multiply(2, [theirs[w] for w in middle], carry)
            near, far = multiply(3, [last, flip(last)], carry)
            held = [near[l] for l in range(pix_size // 2)] + [far[l] for l in range(pix_size // 2)]
            for b in range(pix_bits):
                arrived = None
                for l in reversed([l for l in range(0, pix_size, 1 << b) if l >> b & 1]):
                    piece = held[l]
                    if arrived is not None:
                        piece, arrived = lax.optimization_barrier((piece, arrived))
                        held[l_before ^ 1 << b] = held[l_before ^ 1 << b] + arrived
                    arrived, l_before = between(piece, b), l
                held[l_before ^ 1 << b] = held[l_before ^ 1 << b] + arrived
            return held[0][:-8], held[0][-8]

        def forward(gradient):
            def spread(piece):
                known = {0: piece}
                for b in reversed(range(pix_bits - 1)):
                    for l in list(known):
                        known[l ^ 1 << b] = between(known[l], b)
                return [known[l] for l in range(pix_size // 2)]

            across = between(gradient, pix_bits - 1)
            near = spread(gradient)
            theirs = [place[1, w] for w in range(group)]
            mine = [place[0, w] for w in range(group)]
            *their_near, sums = forward_call(highs, lows, near, index, theirs, chunk_rows, 0, None)
            across, near, their_near = lax.optimization_barrier((across, near, their_near))
            far = spread(across)
            *mine_near, _ = forward_call(highs, lows, near, index, mine, chunk_rows, 0, None)
            half = group // 2
            far, mine_near = lax.optimization_barrier((far, mine_near))

            def finish(far, places, added):
                return forward_call(highs, lows, far, index, places, chunk_rows, 1, (added, sums))

            away, home = slice(half, group), slice(0, half)
            sent_away = flip(finish(far, theirs[away], their_near[away]))
            kept_away = finish(far, mine[away], mine_near[away])
            far, kept_away = lax.optimization_barrier((far, kept_away))
            sent_home = flip(finish(far, theirs[home], their_near[home]))
            kept_home = finish(far, mine[home], mine_near[home])
            held = [kept_home[w] + sent_home[w] for w in range(half)]
            held += [kept_away[w] + sent_away[w] for w in range(group - half)]
            for j in range(stages):
                half = len(held) // 2
                for w in reversed(range(half)):
                    held[w] = held[w] + stage(held[w + half], j)
                held = held[:half]
            return held[0][:-8], held[0][-8]

        gradient, _ = adjoint(observed)
        image, gamma = forward(gradient)
        direction = gradient
        residual = observed
        power = jnp.zeros_like(gradient)
        for step in range(ITERS):
            back, image_squares = adjoint(image)
            alpha = gamma / image_squares
            power = power + alpha * direction
            residual = residual - alpha * image
            gradient = gradient - alpha * back
            if step + 1 < ITERS:
                fresh_image, fresh = forward(gradient)
                beta = fresh / gamma
                image = fresh_image + beta * image
                direction = gradient + beta * direction
                gamma = fresh
        return (power, residual, gradient)

    in_specs = (P("pix", "cell"), P(("pix", "cell"), None))
    out_specs = (P(("cell", "pix"), None), P(("pix", "cell"), None), P(("cell", "pix"), None))
    return jax.shard_map(body, mesh=mesh, in_specs=in_specs, out_specs=out_specs, check_vma=False)
```

```python
import functools

import jax
import jax.numpy as jnp
from jax import lax
from jax.experimental import pallas as pl
from jax.experimental.pallas import tpu as pltpu
from jax.sharding import PartitionSpec as P

ITERS = 2
BLOCK_ROWS = 512
FIRST_LIMIT = 18 * 2**20
LATER_LIMIT = 9 * 2**20
f32 = jnp.float32
bf16 = jnp.bfloat16
f8 = jnp.float8_e4m3fn
RANGE = 224.0 * 256.0
VMEM = pl.BlockSpec(memory_space=pltpu.VMEM)
SMEM = pl.BlockSpec(memory_space=pltpu.SMEM)


def resident(x):
    return pltpu.with_memory_space_constraint(x, pltpu.VMEM)


def split(x):
    high = x.astype(bf16)
    return high, (x - high.astype(f32)).astype(bf16)


def squares(x):
    return jnp.sum(x * x, axis=0, keepdims=True)


def cost(rows, cols, frames, width):
    return pl.CostEstimate(flops=2 * 3 * rows * cols * frames, bytes_accessed=width * rows * cols, transcendentals=0)


def emit_parts(pix, acc, sums, flat_ref, out_ref):
    parts = out_ref.shape[0]
    cells = out_ref.shape[1] - 8
    flat_ref[...] = acc.T
    for part in range(parts):
        start = pl.multiple_of(((pix & (parts - 1)) ^ part) * cells, cells)
        out_ref[part, :cells, :] = flat_ref[pl.ds(start, cells), :]
        out_ref[part, cells:, :] = sums


def first_kernel(count, per_chunk, first, last, index_ref, *refs):
    r_refs, refs = refs[:count], refs[count:]
    near_ref, far_ref, refs = refs[0], refs[1], refs[2:]
    if not first:
        (near_in, far_in, sum_in), refs = refs[:3], refs[3:]
    high_refs, low_refs, scale_ref, refs = refs[:2], refs[2:4], refs[4], refs[5:]
    if last:
        near_out, far_out, near, far, sums, cat_ref, flat_ref = refs
    else:
        near, far, sums, cat_ref = refs
    step = pl.program_id(0)
    frames = r_refs[0].shape[1]
    rows, half = near_ref.shape

    @pl.when(step == 0)
    def _():
        total = jnp.zeros((1, frames), f32)
        for i in range(count):
            r = r_refs[i][...]
            total = total + squares(r)
            for k in range(per_chunk):
                high, low = split(r[k * rows : (k + 1) * rows].T)
                cat_ref[i * per_chunk + k, :frames, :] = high
                cat_ref[i * per_chunk + k, frames:, :] = low
        if first:
            sums[...] = jnp.broadcast_to(total, sums.shape)
            near[...] = jnp.zeros_like(near)
            far[...] = jnp.zeros_like(far)
        else:
            sums[...] = sum_in[...] + total
            near[...] = near_in[...]
            far[...] = far_in[...]

    here = pl.ds(pl.multiple_of(step * rows, rows), rows)
    for k, (ref, acc) in enumerate(((near_ref, near), (far_ref, far))):
        high, low = split(ref[...])
        high_refs[k][here, :] = high
        both = jnp.dot(cat_ref[step], high, preferred_element_type=f32)
        other = jnp.dot(cat_ref[step, :frames, :], low, preferred_element_type=f32)
        largest = jnp.maximum(jnp.max(jnp.max(jnp.abs(high), axis=0, keepdims=True).astype(f32)), 1e-30)
        low_refs[k][...] = (low * (RANGE / largest).astype(bf16)).astype(f8)
        scale_ref[step, k] = largest * (1.0 / RANGE)
        acc[...] += both[:frames] + both[frames:] + other

    if last:

        @pl.when(step == count * per_chunk - 1)
        def _():
            emit_parts(index_ref[0], near[...], sums[...], flat_ref, near_out)
            emit_parts(index_ref[0], far[...], sums[...], flat_ref, far_out)


def blocks(rows, half, per_chunk, base):
    def block(far):
        def where(s, ix):
            return (ix[2 + base + s // per_chunk] * per_chunk + s % per_chunk, ix[1] ^ far)

        return pl.BlockSpec((rows, half), where)

    return [block(0), block(1)]


def first_call(influence, r_parts, index, base, carry, last, parts):
    count = len(r_parts)
    cols = influence.shape[1]
    half = cols // 2
    chunk_rows, frames = r_parts[0].shape
    rows = min(BLOCK_ROWS, chunk_rows)
    per_chunk = chunk_rows // rows
    accs = [((frames, half), f32)] * 2 + [((8, frames), f32)]
    cat = pltpu.VMEM((count * per_chunk, 2 * frames, rows), bf16)
    out_shape = [
        *[pltpu.VMEM((count * chunk_rows, half), bf16)] * 2,
        *[pltpu.HBM((count * chunk_rows, half), f8)] * 2,
        jax.ShapeDtypeStruct((count * per_chunk, 2), f32),
    ]
    if last:
        out_shape += [jax.ShapeDtypeStruct((parts // 2, half // (parts // 2) + 8, frames), f32)] * 2
        scratch = [pltpu.VMEM(*a) for a in accs] + [cat, pltpu.VMEM((half, frames), f32)]
    else:
        out_shape += [jax.ShapeDtypeStruct(*a) for a in accs]
        scratch = [cat]
    high_near, high_far, low_near, low_far, scale, *rest = pl.pallas_call(
        functools.partial(first_kernel, count, per_chunk, carry is None, last),
        grid_spec=pltpu.PrefetchScalarGridSpec(
            num_scalar_prefetch=1,
            grid=(count * per_chunk,),
            in_specs=[VMEM] * count + blocks(rows, half, per_chunk, base) + [VMEM] * (0 if carry is None else 3),
            out_specs=[VMEM] * 2 + [pl.BlockSpec((rows, half), lambda s, ix: (s, 0))] * 2 + [SMEM] + [VMEM] * (len(out_shape) - 5),
            scratch_shapes=scratch,
        ),
        out_shape=out_shape,
        compiler_params=pltpu.CompilerParams(vmem_limit_bytes=FIRST_LIMIT),
        cost_estimate=cost(count * chunk_rows, cols, frames, 4),
        name="first_adjoint",
    )(index, *r_parts, influence, influence, *(() if carry is None else carry))
    return (high_near, high_far), (low_near, low_far, scale), rest


def adjoint_kernel(count, sides, last, index_ref, *refs):
    halves = len(sides)
    r_refs, refs = refs[:count], refs[count:]
    high_refs, low_refs, scale_ref, refs = refs[:halves], refs[halves : 2 * halves], refs[2 * halves], refs[2 * halves + 1 :]
    accs_in, sum_in, refs = refs[:halves], refs[halves], refs[halves + 1 :]
    if last:
        outs, refs = refs[:1], refs[1:]
    else:
        outs, sum_out, refs = refs[:halves], refs[halves], refs[halves + 1 :]
    cat_ref, scaled_ref = refs[:2]
    chunk_rows, frames = r_refs[0].shape
    rows = cat_ref.shape[1] // scale_ref.shape[0]
    total = sum_in[...]
    for i in range(count):
        r = r_refs[i][...]
        total = total + squares(r)
        turned = r.T
        high, low = split(turned)
        here = slice(i * chunk_rows, (i + 1) * chunk_rows)
        cat_ref[:frames, here] = high
        cat_ref[frames:, here] = low
        for b in range(chunk_rows // rows):
            at = i * chunk_rows + b * rows
            for k in range(halves):
                scale = scale_ref[at // rows, sides[k]]
                scaled_ref[k, :, at : at + rows] = (turned[:, b * rows : (b + 1) * rows] * scale).astype(bf16)
    for k in range(halves):
        both = jnp.dot(cat_ref[...], high_refs[k][...], preferred_element_type=f32)
        acc = accs_in[k][...] + both[:frames] + both[frames:]
        acc = acc + jnp.dot(scaled_ref[k], low_refs[k][...].astype(bf16), preferred_element_type=f32)
        if last:
            emit_parts(index_ref[0], acc, total, refs[2], outs[0])
        else:
            outs[k][...] = acc
    if not last:
        sum_out[...] = total


def adjoint_call(high, low, r_parts, index, carry, sides, last, parts):
    count = len(r_parts)
    rows = high[0].shape[0]
    halves = len(sides)
    half = carry[0].shape[1]
    frames = r_parts[0].shape[1]
    scratch = [
        pltpu.VMEM((2 * frames, rows), bf16),
        pltpu.VMEM((halves, frames, rows), bf16),
    ]
    if last:
        out_shape = jax.ShapeDtypeStruct((parts // 2, half // (parts // 2) + 8, frames), f32)
        out_specs = VMEM
        scratch.append(pltpu.VMEM((half, frames), f32))
    else:
        out_shape = [jax.ShapeDtypeStruct(c.shape, f32) for c in carry]
        out_specs = [VMEM] * (halves + 1)
    return pl.pallas_call(
        functools.partial(adjoint_kernel, count, sides, last),
        in_specs=[SMEM] + [VMEM] * (count + 2 * halves) + [SMEM] + [VMEM] * (halves + 1),
        out_specs=out_specs,
        out_shape=out_shape,
        scratch_shapes=scratch,
        compiler_params=pltpu.CompilerParams(vmem_limit_bytes=LATER_LIMIT),
        cost_estimate=cost(rows, halves * half, frames, 2),
        name="adjoint_product",
    )(
        index,
        *r_parts,
        *[resident(high[k]) for k in sides],
        *[resident(low[k]) for k in sides],
        low[2],
        *carry,
    )


def forward_kernel(parts, arrays, places, side, chunk_rows, near, index_ref, *refs):
    x_refs, refs = refs[:parts], refs[parts:]
    highs, lows, scales, refs = refs[:arrays], refs[arrays : 2 * arrays], refs[2 * arrays : 3 * arrays], refs[3 * arrays :]
    count = len(places)
    if not near:
        added, sum_in, refs = refs[:count], refs[count], refs[count + 1 :]
    if near:
        outs, sum_out, refs = refs[:count], refs[count], refs[count + 1 :]
    else:
        outs, refs = [refs[0].at[i] for i in range(count)], refs[1:]
    (cat_ref,) = refs
    cells, frames = x_refs[0].shape
    total = jnp.zeros((1, frames), f32)
    for part in range(parts):
        x = x_refs[part][...]
        high, low = split(x)
        start = pl.multiple_of(((index_ref[0] & (parts - 1)) ^ part) * cells, cells)
        cat_ref[pl.ds(start, cells), :frames] = high
        cat_ref[pl.ds(start, cells), frames:] = low
        total = total + squares(x)
    if near:
        sum_out[...] = jnp.broadcast_to(total, sum_out.shape)
    for i, (which, row) in enumerate(places):
        both = jnp.dot(highs[which][row : row + chunk_rows, :], cat_ref[...], preferred_element_type=f32)
        value = both[:, :frames] + both[:, frames:]
        other = jnp.dot(lows[which][row : row + chunk_rows, :].astype(bf16), cat_ref[:, :frames], preferred_element_type=f32)
        rows = highs[which].shape[0] // scales[which].shape[0]
        for start in range(0, chunk_rows, rows):
            at = slice(start, start + rows)
            whole = value[at] + other[at] * scales[which][(row + start) // rows, side]
            outs[i][at, :] = whole if near else whole + added[i][at, :]
        if not near:
            outs[i][chunk_rows:, :] = sum_in[...] + total


def forward_call(highs, lows, x_parts, index, places, chunk_rows, side, added):
    count = len(places)
    used = sorted({g for g, _ in places})
    slots = [(used.index(g), row) for g, row in places]
    cells, frames = x_parts[0].shape
    half = cells * len(x_parts)
    near = added is None
    extra = [] if near else [*added[0], added[1]]
    rows = chunk_rows if near else chunk_rows + 8
    if near:
        out_shape = [jax.ShapeDtypeStruct((rows, frames), f32)] * count + [jax.ShapeDtypeStruct((8, frames), f32)]
    else:
        out_shape = [jax.ShapeDtypeStruct((count, rows, frames), f32)]
    result = pl.pallas_call(
        functools.partial(forward_kernel, len(x_parts), len(used), slots, side, chunk_rows, near),
        in_specs=[SMEM]
        + [VMEM] * (len(x_parts) + len(used))
        + [VMEM] * len(used)
        + [SMEM] * len(used)
        + [VMEM] * len(extra),
        out_specs=[VMEM] * len(out_shape),
        out_shape=out_shape,
        scratch_shapes=[
            pltpu.VMEM((half, 2 * frames), bf16),
        ],
        compiler_params=pltpu.CompilerParams(vmem_limit_bytes=LATER_LIMIT),
        cost_estimate=cost(count * chunk_rows, half, frames, 2),
        name="forward_product",
    )(
        index,
        *x_parts,
        *[resident(highs[g][side]) for g in used],
        *[resident(lows[g][side]) for g in used],
        *[lows[g][2] for g in used],
        *extra,
    )
    return result if near else result[0]


def solution(mesh):
    cell_size, pix_size = mesh.shape["cell"], mesh.shape["pix"]
    bits = cell_size.bit_length() - 1
    stages = bits - 1
    group = cell_size // 2
    order = (list(range(1, bits)), list(range(bits - 1, 0, -1)))

    def offset(core, w):
        return sum(1 << order[core][j] for j in range(stages) if (w >> (stages - 1 - j)) & 1)

    stage_perm = [[(i, i ^ (1 << order[i & 1][j])) for i in range(cell_size)] for j in range(stages)]
    core_perm = [(i, i ^ 1) for i in range(cell_size)]
    pix_bits = pix_size.bit_length() - 1
    pix_perm = [[(i, i ^ (1 << b)) for i in range(pix_size)] for b in range(pix_bits)]
    middle = range(1, group - 1)
    groups = [[(0, 0), (1, 0)], [(0, w) for w in middle], [(1, w) for w in middle], [(0, group - 1), (1, group - 1)]]

    starts = [sum(map(len, groups[:g])) for g in range(len(groups))]
    uses = [[offset(core ^ c, w) ^ c for members in groups for c, w in members] for core in range(2)]

    def body(influence, observed):
        chunk_rows = influence.shape[0] // cell_size
        me_cell, me_pix = lax.axis_index("cell"), lax.axis_index("pix")
        order_of_use = jnp.where((me_cell & 1) == 0, jnp.array(uses[0], jnp.int32), jnp.array(uses[1], jnp.int32))
        index = jnp.concatenate([jnp.stack([me_pix, me_pix // (pix_size // 2)]), me_cell ^ order_of_use])
        place = {c: (g, i * chunk_rows) for g, members in enumerate(groups) for i, c in enumerate(members)}
        highs, lows = [], []

        def stage(piece, j):
            return lax.ppermute(piece, "cell", stage_perm[j])

        def flip(piece):
            return lax.ppermute(piece, "cell", core_perm)

        def between(piece, b):
            return lax.ppermute(piece, "pix", pix_perm[b])

        def adjoint(residual):
            half = influence.shape[1] // 2
            first = not highs
            carry = None if first else [
                jnp.zeros((residual.shape[1], half), f32),
                jnp.zeros((residual.shape[1], half), f32),
                jnp.zeros((8, residual.shape[1]), f32),
            ]

            def multiply(g, pieces, carry):
                if first:
                    high, low, carry = first_call(
                        influence, pieces, index, starts[g], carry, g == len(groups) - 1, pix_size
                    )
                    highs.append(high)
                    lows.append(low)
                    return carry
                return adjoint_call(highs[g], lows[g], pieces, index, carry, (0, 1), False, pix_size)

            def finish(pieces, carry, side):
                carry = adjoint_call(highs[2], lows[2], pieces[0], index, carry, (side,), False, pix_size)
                return adjoint_call(highs[3], lows[3], pieces[1], index, carry, (side,), True, pix_size)

            mine = [residual]
            for j in reversed(range(1, stages)):
                mine = mine + [stage(piece, j) for piece in mine]
            early = stage(residual, 0) if first else None
            carry = multiply(0, [residual, flip(residual)], carry)
            late, carry = lax.optimization_barrier((residual, carry))
            crossed = early if first else stage(late, 0)
            rest, carry = lax.optimization_barrier((mine[1:], carry))
            mine = [residual, *rest, crossed, *[stage(piece, 0) for piece in rest]]
            theirs = [None] + [flip(piece) for piece in mine[1 : group - 1]]
            carry = multiply(1, [mine[w] for w in middle], carry)
            last, carry = lax.optimization_barrier((mine[group - 1], carry))
            pieces = [theirs[w] for w in middle], [last, flip(last)]
            if first:
                near, far = multiply(3, pieces[1], multiply(2, pieces[0], carry))
            else:
                far = finish(pieces, [carry[1], carry[2]], 1)
                far, carry = lax.optimization_barrier((far, carry))
                near = finish(pieces, [carry[0], carry[2]], 0)
            held = [near[l] for l in range(pix_size // 2)] + [far[l] for l in range(pix_size // 2)]
            for b in range(pix_bits):
                arrived = None
                for l in reversed([l for l in range(0, pix_size, 1 << b) if l >> b & 1]):
                    piece = held[l]
                    if arrived is not None:
                        piece, arrived = lax.optimization_barrier((piece, arrived))
                        held[l_before ^ 1 << b] = held[l_before ^ 1 << b] + arrived
                    arrived, l_before = between(piece, b), l
                held[l_before ^ 1 << b] = held[l_before ^ 1 << b] + arrived
            return held[0][:-8], held[0][-8]

        def forward(gradient):
            def spread(piece):
                known = {0: piece}
                for b in reversed(range(pix_bits - 1)):
                    for l in list(known):
                        known[l ^ 1 << b] = between(known[l], b)
                return [known[l] for l in range(pix_size // 2)]

            across = between(gradient, pix_bits - 1)
            near = spread(gradient)
            theirs = [place[1, w] for w in range(group)]
            mine = [place[0, w] for w in range(group)]
            *their_near, sums = forward_call(highs, lows, near, index, theirs, chunk_rows, 0, None)
            across, near, their_near = lax.optimization_barrier((across, near, their_near))
            far = spread(across)
            *mine_near, _ = forward_call(highs, lows, near, index, mine, chunk_rows, 0, None)
            half = group // 2
            far, mine_near = lax.optimization_barrier((far, mine_near))

            def finish(far, places, added):
                return forward_call(highs, lows, far, index, places, chunk_rows, 1, (added, sums))

            away, home = slice(half, group), slice(0, half)
            sent_away = flip(finish(far, theirs[away], their_near[away]))
            kept_away = finish(far, mine[away], mine_near[away])
            far, kept_away = lax.optimization_barrier((far, kept_away))
            sent_home = flip(finish(far, theirs[home], their_near[home]))
            kept_home = finish(far, mine[home], mine_near[home])
            held = [kept_home[w] + sent_home[w] for w in range(half)]
            held += [kept_away[w] + sent_away[w] for w in range(group - half)]
            for j in range(stages):
                half = len(held) // 2
                for w in reversed(range(half)):
                    held[w] = held[w] + stage(held[w + half], j)
                held = held[:half]
            return held[0][:-8], held[0][-8]

        gradient, _ = adjoint(observed)
        image, gamma = forward(gradient)
        direction = gradient
        residual = observed
        power = jnp.zeros_like(gradient)
        for step in range(ITERS):
            back, image_squares = adjoint(image)
            alpha = gamma / image_squares
            power = power + alpha * direction
            residual = residual - alpha * image
            gradient = gradient - alpha * back
            if step + 1 < ITERS:
                fresh_image, fresh = forward(gradient)
                beta = fresh / gamma
                image = fresh_image + beta * image
                direction = gradient + beta * direction
                gamma = fresh
        return (power, residual, gradient)

    in_specs = (P("pix", "cell"), P(("pix", "cell"), None))
    out_specs = (P(("cell", "pix"), None), P(("pix", "cell"), None), P(("cell", "pix"), None))
    return jax.shard_map(body, mesh=mesh, in_specs=in_specs, out_specs=out_specs, check_vma=False)
```

```python
import functools

import jax
import jax.numpy as jnp
from jax import lax
from jax.experimental import pallas as pl
from jax.experimental.pallas import tpu as pltpu
from jax.sharding import PartitionSpec as P

ITERS = 2
BLOCK_ROWS = 512
FIRST_LIMIT = 20 * 2**20
LATER_LIMIT = 9 * 2**20
f32 = jnp.float32
bf16 = jnp.bfloat16
f8 = jnp.float8_e4m3fn
RANGE = 224.0 * 256.0
VMEM = pl.BlockSpec(memory_space=pltpu.VMEM)
SMEM = pl.BlockSpec(memory_space=pltpu.SMEM)


def resident(x):
    return pltpu.with_memory_space_constraint(x, pltpu.VMEM)


def split(x):
    high = x.astype(bf16)
    return high, (x - high.astype(f32)).astype(bf16)


def squares(x):
    return jnp.sum(x * x, axis=0, keepdims=True)


def cost(rows, cols, frames, width):
    return pl.CostEstimate(flops=2 * 3 * rows * cols * frames, bytes_accessed=width * rows * cols, transcendentals=0)


def emit_parts(pix, acc, sums, flat_ref, out_ref):
    parts = out_ref.shape[0]
    cells = out_ref.shape[1] - 8
    flat_ref[...] = acc.T
    for part in range(parts):
        start = pl.multiple_of(((pix & (parts - 1)) ^ part) * cells, cells)
        out_ref[part, :cells, :] = flat_ref[pl.ds(start, cells), :]
        out_ref[part, cells:, :] = sums


def first_kernel(count, per_chunk, first, last, index_ref, *refs):
    r_refs, refs = refs[:count], refs[count:]
    near_ref, far_ref, refs = refs[0], refs[1], refs[2:]
    if not first:
        (near_in, far_in, sum_in), refs = refs[:3], refs[3:]
    high_refs, low_refs, scale_ref, refs = refs[:2], refs[2:4], refs[4], refs[5:]
    if last:
        near_out, far_out, near, far, sums, cat_ref, flat_ref = refs
    else:
        near, far, sums, cat_ref = refs
    step = pl.program_id(0)
    frames = r_refs[0].shape[1]
    rows, half = near_ref.shape

    @pl.when(step == 0)
    def _():
        total = jnp.zeros((1, frames), f32)
        for i in range(count):
            r = r_refs[i][...]
            total = total + squares(r)
            for k in range(per_chunk):
                high, low = split(r[k * rows : (k + 1) * rows].T)
                cat_ref[i * per_chunk + k, :frames, :] = high
                cat_ref[i * per_chunk + k, frames:, :] = low
        if first:
            sums[...] = jnp.broadcast_to(total, sums.shape)
            near[...] = jnp.zeros_like(near)
            far[...] = jnp.zeros_like(far)
        else:
            sums[...] = sum_in[...] + total
            near[...] = near_in[...]
            far[...] = far_in[...]

    here = pl.ds(pl.multiple_of(step * rows, rows), rows)
    for k, (ref, acc) in enumerate(((near_ref, near), (far_ref, far))):
        high, low = split(ref[...])
        high_refs[k][here, :] = high
        both = jnp.dot(cat_ref[step], high, preferred_element_type=f32)
        other = jnp.dot(cat_ref[step, :frames, :], low, preferred_element_type=f32)
        largest = jnp.maximum(jnp.max(jnp.max(jnp.abs(high), axis=0, keepdims=True).astype(f32)), 1e-30)
        low_refs[k][...] = (low * (RANGE / largest).astype(bf16)).astype(f8)
        scale_ref[step, k] = largest * (1.0 / RANGE)
        acc[...] += both[:frames] + both[frames:] + other

    if last:

        @pl.when(step == count * per_chunk - 1)
        def _():
            emit_parts(index_ref[0], near[...], sums[...], flat_ref, near_out)
            emit_parts(index_ref[0], far[...], sums[...], flat_ref, far_out)


def blocks(rows, half, per_chunk, base):
    def block(far):
        def where(s, ix):
            return (ix[2 + base + s // per_chunk] * per_chunk + s % per_chunk, ix[1] ^ far)

        return pl.BlockSpec((rows, half), where)

    return [block(0), block(1)]


def first_call(influence, r_parts, index, base, carry, last, parts):
    count = len(r_parts)
    cols = influence.shape[1]
    half = cols // 2
    chunk_rows, frames = r_parts[0].shape
    rows = min(BLOCK_ROWS, chunk_rows)
    per_chunk = chunk_rows // rows
    accs = [((frames, half), f32)] * 2 + [((8, frames), f32)]
    cat = pltpu.VMEM((count * per_chunk, 2 * frames, rows), bf16)
    out_shape = [
        *[pltpu.VMEM((count * chunk_rows, half), bf16)] * 2,
        *[pltpu.HBM((count * chunk_rows, half), f8)] * 2,
        jax.ShapeDtypeStruct((count * per_chunk, 2), f32),
    ]
    if last:
        out_shape += [jax.ShapeDtypeStruct((parts // 2, half // (parts // 2) + 8, frames), f32)] * 2
        scratch = [pltpu.VMEM(*a) for a in accs] + [cat, pltpu.VMEM((half, frames), f32)]
    else:
        out_shape += [jax.ShapeDtypeStruct(*a) for a in accs]
        scratch = [cat]
    high_near, high_far, low_near, low_far, scale, *rest = pl.pallas_call(
        functools.partial(first_kernel, count, per_chunk, carry is None, last),
        grid_spec=pltpu.PrefetchScalarGridSpec(
            num_scalar_prefetch=1,
            grid=(count * per_chunk,),
            in_specs=[VMEM] * count + blocks(rows, half, per_chunk, base) + [VMEM] * (0 if carry is None else 3),
            out_specs=[VMEM] * 2 + [pl.BlockSpec((rows, half), lambda s, ix: (s, 0))] * 2 + [SMEM] + [VMEM] * (len(out_shape) - 5),
            scratch_shapes=scratch,
        ),
        out_shape=out_shape,
        compiler_params=pltpu.CompilerParams(vmem_limit_bytes=FIRST_LIMIT),
        cost_estimate=cost(count * chunk_rows, cols, frames, 4),
        name="first_adjoint",
    )(index, *r_parts, influence, influence, *(() if carry is None else carry))
    return (high_near, high_far), (low_near, low_far, scale), rest


def adjoint_kernel(count, sides, last, index_ref, *refs):
    halves = len(sides)
    r_refs, refs = refs[:count], refs[count:]
    high_refs, low_refs, scale_ref, refs = refs[:halves], refs[halves : 2 * halves], refs[2 * halves], refs[2 * halves + 1 :]
    accs_in, sum_in, refs = refs[:halves], refs[halves], refs[halves + 1 :]
    if last:
        outs, refs = refs[:1], refs[1:]
    else:
        outs, sum_out, refs = refs[:halves], refs[halves], refs[halves + 1 :]
    cat_ref, scaled_ref = refs[:2]
    chunk_rows, frames = r_refs[0].shape
    rows = cat_ref.shape[1] // scale_ref.shape[0]
    total = sum_in[...]
    for i in range(count):
        r = r_refs[i][...]
        total = total + squares(r)
        turned = r.T
        high, low = split(turned)
        here = slice(i * chunk_rows, (i + 1) * chunk_rows)
        cat_ref[:frames, here] = high
        cat_ref[frames:, here] = low
        for b in range(chunk_rows // rows):
            at = i * chunk_rows + b * rows
            for k in range(halves):
                scale = scale_ref[at // rows, sides[k]]
                scaled_ref[k, :, at : at + rows] = (turned[:, b * rows : (b + 1) * rows] * scale).astype(bf16)
    for k in range(halves):
        both = jnp.dot(cat_ref[...], high_refs[k][...], preferred_element_type=f32)
        acc = accs_in[k][...] + both[:frames] + both[frames:]
        acc = acc + jnp.dot(scaled_ref[k], low_refs[k][...].astype(bf16), preferred_element_type=f32)
        if last:
            emit_parts(index_ref[0], acc, total, refs[2], outs[0])
        else:
            outs[k][...] = acc
    if not last:
        sum_out[...] = total


def adjoint_call(high, low, r_parts, index, carry, sides, last, parts):
    count = len(r_parts)
    rows = high[0].shape[0]
    halves = len(sides)
    half = carry[0].shape[1]
    frames = r_parts[0].shape[1]
    scratch = [
        pltpu.VMEM((2 * frames, rows), bf16),
        pltpu.VMEM((halves, frames, rows), bf16),
    ]
    if last:
        out_shape = jax.ShapeDtypeStruct((parts // 2, half // (parts // 2) + 8, frames), f32)
        out_specs = VMEM
        scratch.append(pltpu.VMEM((half, frames), f32))
    else:
        out_shape = [jax.ShapeDtypeStruct(c.shape, f32) for c in carry]
        out_specs = [VMEM] * (halves + 1)
    return pl.pallas_call(
        functools.partial(adjoint_kernel, count, sides, last),
        in_specs=[SMEM] + [VMEM] * (count + 2 * halves) + [SMEM] + [VMEM] * (halves + 1),
        out_specs=out_specs,
        out_shape=out_shape,
        scratch_shapes=scratch,
        compiler_params=pltpu.CompilerParams(vmem_limit_bytes=LATER_LIMIT),
        cost_estimate=cost(rows, halves * half, frames, 2),
        name="adjoint_product",
    )(
        index,
        *r_parts,
        *[resident(high[k]) for k in sides],
        *[resident(low[k]) for k in sides],
        low[2],
        *carry,
    )


def forward_kernel(parts, arrays, places, side, chunk_rows, near, index_ref, *refs):
    x_refs, refs = refs[:parts], refs[parts:]
    highs, lows, scales, refs = refs[:arrays], refs[arrays : 2 * arrays], refs[2 * arrays : 3 * arrays], refs[3 * arrays :]
    count = len(places)
    if not near:
        added, sum_in, refs = refs[:count], refs[count], refs[count + 1 :]
    if near:
        outs, sum_out, refs = refs[:count], refs[count], refs[count + 1 :]
    else:
        outs, refs = [refs[0].at[i] for i in range(count)], refs[1:]
    (cat_ref,) = refs
    cells, frames = x_refs[0].shape
    total = jnp.zeros((1, frames), f32)
    for part in range(parts):
        x = x_refs[part][...]
        high, low = split(x)
        start = pl.multiple_of(((index_ref[0] & (parts - 1)) ^ part) * cells, cells)
        cat_ref[pl.ds(start, cells), :frames] = high
        cat_ref[pl.ds(start, cells), frames:] = low
        total = total + squares(x)
    top = x_refs[0][...]
    top = jnp.max(jnp.abs(top), axis=0, keepdims=True)
    for part in range(1, parts):
        top = jnp.maximum(top, jnp.max(jnp.abs(x_refs[part][...]), axis=0, keepdims=True))
    top = jnp.maximum(top, 1e-30)
    narrow = (cat_ref[:, :frames].astype(f32) * (224.0 / top)).astype(f8)
    widen = top * (1.0 / 224.0)
    if near:
        sum_out[...] = jnp.broadcast_to(total, sum_out.shape)
    for i, (which, row) in enumerate(places):
        both = jnp.dot(highs[which][row : row + chunk_rows, :], cat_ref[...], preferred_element_type=f32)
        value = both[:, :frames] + both[:, frames:]
        other = jnp.dot(lows[which][row : row + chunk_rows, :], narrow, preferred_element_type=f32) * widen
        rows = highs[which].shape[0] // scales[which].shape[0]
        for start in range(0, chunk_rows, rows):
            at = slice(start, start + rows)
            whole = value[at] + other[at] * scales[which][(row + start) // rows, side]
            outs[i][at, :] = whole if near else whole + added[i][at, :]
        if not near:
            outs[i][chunk_rows:, :] = sum_in[...] + total


def forward_call(highs, lows, x_parts, index, places, chunk_rows, side, added):
    count = len(places)
    used = sorted({g for g, _ in places})
    slots = [(used.index(g), row) for g, row in places]
    cells, frames = x_parts[0].shape
    half = cells * len(x_parts)
    near = added is None
    extra = [] if near else [*added[0], added[1]]
    rows = chunk_rows if near else chunk_rows + 8
    if near:
        out_shape = [jax.ShapeDtypeStruct((rows, frames), f32)] * count + [jax.ShapeDtypeStruct((8, frames), f32)]
    else:
        out_shape = [jax.ShapeDtypeStruct((count, rows, frames), f32)]
    result = pl.pallas_call(
        functools.partial(forward_kernel, len(x_parts), len(used), slots, side, chunk_rows, near),
        in_specs=[SMEM]
        + [VMEM] * (len(x_parts) + len(used))
        + [VMEM] * len(used)
        + [SMEM] * len(used)
        + [VMEM] * len(extra),
        out_specs=[VMEM] * len(out_shape),
        out_shape=out_shape,
        scratch_shapes=[
            pltpu.VMEM((half, 2 * frames), bf16),
        ],
        compiler_params=pltpu.CompilerParams(vmem_limit_bytes=LATER_LIMIT),
        cost_estimate=cost(count * chunk_rows, half, frames, 2),
        name="forward_product",
    )(
        index,
        *x_parts,
        *[resident(highs[g][side]) for g in used],
        *[resident(lows[g][side]) for g in used],
        *[lows[g][2] for g in used],
        *extra,
    )
    return result if near else result[0]


def solution(mesh):
    cell_size, pix_size = mesh.shape["cell"], mesh.shape["pix"]
    bits = cell_size.bit_length() - 1
    stages = bits - 1
    group = cell_size // 2
    order = (list(range(1, bits)), list(range(bits - 1, 0, -1)))

    def offset(core, w):
        return sum(1 << order[core][j] for j in range(stages) if (w >> (stages - 1 - j)) & 1)

    stage_perm = [[(i, i ^ (1 << order[i & 1][j])) for i in range(cell_size)] for j in range(stages)]
    core_perm = [(i, i ^ 1) for i in range(cell_size)]
    pix_bits = pix_size.bit_length() - 1
    pix_perm = [[(i, i ^ (1 << b)) for i in range(pix_size)] for b in range(pix_bits)]
    middle = range(1, group - 1)
    groups = [[(0, 0), (1, 0)], [(0, w) for w in middle], [(1, w) for w in middle], [(0, group - 1), (1, group - 1)]]

    starts = [sum(map(len, groups[:g])) for g in range(len(groups))]
    uses = [[offset(core ^ c, w) ^ c for members in groups for c, w in members] for core in range(2)]

    def body(influence, observed):
        chunk_rows = influence.shape[0] // cell_size
        me_cell, me_pix = lax.axis_index("cell"), lax.axis_index("pix")
        order_of_use = jnp.where((me_cell & 1) == 0, jnp.array(uses[0], jnp.int32), jnp.array(uses[1], jnp.int32))
        index = jnp.concatenate([jnp.stack([me_pix, me_pix // (pix_size // 2)]), me_cell ^ order_of_use])
        place = {c: (g, i * chunk_rows) for g, members in enumerate(groups) for i, c in enumerate(members)}
        highs, lows = [], []

        def stage(piece, j):
            return lax.ppermute(piece, "cell", stage_perm[j])

        def flip(piece):
            return lax.ppermute(piece, "cell", core_perm)

        def between(piece, b):
            return lax.ppermute(piece, "pix", pix_perm[b])

        def adjoint(residual):
            half = influence.shape[1] // 2
            first = not highs
            carry = None if first else [
                jnp.zeros((residual.shape[1], half), f32),
                jnp.zeros((residual.shape[1], half), f32),
                jnp.zeros((8, residual.shape[1]), f32),
            ]

            def multiply(g, pieces, carry):
                if first:
                    high, low, carry = first_call(
                        influence, pieces, index, starts[g], carry, g == len(groups) - 1, pix_size
                    )
                    highs.append(high)
                    lows.append(low)
                    return carry
                return adjoint_call(highs[g], lows[g], pieces, index, carry, (0, 1), False, pix_size)

            def finish(pieces, carry, side):
                carry = adjoint_call(highs[2], lows[2], pieces[0], index, carry, (side,), False, pix_size)
                return adjoint_call(highs[3], lows[3], pieces[1], index, carry, (side,), True, pix_size)

            mine = [residual]
            for j in reversed(range(1, stages)):
                mine = mine + [stage(piece, j) for piece in mine]
            early = stage(residual, 0) if first else None
            carry = multiply(0, [residual, flip(residual)], carry)
            late, carry = lax.optimization_barrier((residual, carry))
            crossed = early if first else stage(late, 0)
            rest, carry = lax.optimization_barrier((mine[1:], carry))
            mine = [residual, *rest, crossed, *[stage(piece, 0) for piece in rest]]
            theirs = [None] + [flip(piece) for piece in mine[1 : group - 1]]
            carry = multiply(1, [mine[w] for w in middle], carry)
            last, carry = lax.optimization_barrier((mine[group - 1], carry))
            pieces = [theirs[w] for w in middle], [last, flip(last)]
            if first:
                near, far = multiply(3, pieces[1], multiply(2, pieces[0], carry))
            else:
                far = finish(pieces, [carry[1], carry[2]], 1)
                far, carry = lax.optimization_barrier((far, carry))
                near = finish(pieces, [carry[0], carry[2]], 0)
            held = [near[l] for l in range(pix_size // 2)] + [far[l] for l in range(pix_size // 2)]
            for b in range(pix_bits):
                arrived = None
                for l in reversed([l for l in range(0, pix_size, 1 << b) if l >> b & 1]):
                    piece = held[l]
                    if arrived is not None:
                        piece, arrived = lax.optimization_barrier((piece, arrived))
                        held[l_before ^ 1 << b] = held[l_before ^ 1 << b] + arrived
                    arrived, l_before = between(piece, b), l
                held[l_before ^ 1 << b] = held[l_before ^ 1 << b] + arrived
            return held[0][:-8], held[0][-8]

        def forward(gradient):
            def spread(piece):
                known = {0: piece}
                for b in reversed(range(pix_bits - 1)):
                    for l in list(known):
                        known[l ^ 1 << b] = between(known[l], b)
                return [known[l] for l in range(pix_size // 2)]

            across = between(gradient, pix_bits - 1)
            near = spread(gradient)
            theirs = [place[1, w] for w in range(group)]
            mine = [place[0, w] for w in range(group)]
            *their_near, sums = forward_call(highs, lows, near, index, theirs, chunk_rows, 0, None)
            across, near, their_near = lax.optimization_barrier((across, near, their_near))
            far = spread(across)
            *mine_near, _ = forward_call(highs, lows, near, index, mine, chunk_rows, 0, None)
            half = group // 2
            far, mine_near = lax.optimization_barrier((far, mine_near))

            def finish(far, places, added):
                return forward_call(highs, lows, far, index, places, chunk_rows, 1, (added, sums))

            away, home = slice(half, group), slice(0, half)
            sent_away = flip(finish(far, theirs[away], their_near[away]))
            kept_away = finish(far, mine[away], mine_near[away])
            far, kept_away = lax.optimization_barrier((far, kept_away))
            sent_home = flip(finish(far, theirs[home], their_near[home]))
            kept_home = finish(far, mine[home], mine_near[home])
            held = [kept_home[w] + sent_home[w] for w in range(half)]
            held += [kept_away[w] + sent_away[w] for w in range(group - half)]
            for j in range(stages):
                half = len(held) // 2
                for w in reversed(range(half)):
                    held[w] = held[w] + stage(held[w + half], j)
                held = held[:half]
            return held[0][:-8], held[0][-8]

        gradient, _ = adjoint(observed)
        image, gamma = forward(gradient)
        direction = gradient
        residual = observed
        power = jnp.zeros_like(gradient)
        for step in range(ITERS):
            back, image_squares = adjoint(image)
            alpha = gamma / image_squares
            power = power + alpha * direction
            residual = residual - alpha * image
            gradient = gradient - alpha * back
            if step + 1 < ITERS:
                fresh_image, fresh = forward(gradient)
                beta = fresh / gamma
                image = fresh_image + beta * image
                direction = gradient + beta * direction
                gamma = fresh
        return (power, residual, gradient)

    in_specs = (P("pix", "cell"), P(("pix", "cell"), None))
    out_specs = (P(("cell", "pix"), None), P(("pix", "cell"), None), P(("cell", "pix"), None))
    return jax.shard_map(body, mesh=mesh, in_specs=in_specs, out_specs=out_specs, check_vma=False)
```
